512 devices in a mesh: band: 128 (over z, y, core), mode: 4 (over x).
Axes of the slice: x: 4, y: 4, z: 16, core: 2. Of those that a mesh axis runs over, the one named last changes fastest.
Arguments:
- velocity: bfloat16 [1, 131072, 1024], P(None, ('band', 'mode')), may hold values from -6 to 6
- radiation_modes: bfloat16 [131072, 1024], P('band', 'mode'), may hold values from -0.03125 to 0.03125
- resistance: float32 [128, 1024, 1024], P('band', None, 'mode'), as said below
- mode_ranks: int32 [128], P('band'), may hold values from 128 to 1024, as said below
- freq_table: int32 [512], replicated, may hold values from 0 to 511, each once
Outputs:
- adjoint_force: bfloat16 [1, 131072, 1024], P(None, ('band', 'mode'))
The draws below stay inside these ranges and needn't reach their ends.
Inputs may be any that keep to these rules, and one draw needn't show every extreme that they name: `resistance`: each band's matrix is symmetric. `mode_ranks`: the ranks never fall with the band index; the first band keeps 1024 // 8 modes and the last 1024.
All inputs are finite; a program needn't handle non-finite values.
Results may differ from the reference program's by a relative error of at most 0.015.
Values may be sent and summed in bfloat16 or wider, within the bound.
No kernel may reach another device: no remote copies, remote signals or barrier semaphores. Data moves between devices by JAX's collectives and lax.ppermute only.
A program may use at most 64 MiB of HBM per device.

```python
import math
import jax
import jax.numpy as jnp
from jax import lax

WIN = 1
NT = 1024
F = 512
RMAX = 1024
PATCHES = 131072
NBANDS = 128
FPB = 4


def draw_resistance(key, part):
    first_key, second_key = jax.random.split(jax.random.fold_in(key, 11))
    noise = jax.random.normal(first_key, (NBANDS, RMAX, RMAX), jnp.float32)
    symmetric = (noise + jnp.swapaxes(noise, 1, 2)) * (0.5 / jnp.sqrt(jnp.float32(RMAX)))
    diagonal_part = jax.random.uniform(second_key, (NBANDS, RMAX), jnp.float32, 0.5, 2.0)
    identity = jnp.eye(RMAX, dtype=jnp.float32)
    return symmetric + diagonal_part[:, :, None] * identity[None, :, :]


def draw_mode_ranks(key, part):
    drawn = jax.random.randint(jax.random.fold_in(key, 23), (NBANDS,), RMAX // 8, RMAX + 1, jnp.int32)
    ordered = jnp.sort(drawn)
    ordered = ordered.at[0].set(RMAX // 8)
    ordered = ordered.at[NBANDS - 1].set(RMAX)
    return ordered.astype(jnp.int32)


def level_of(key, extent, cuts, least, top_value):
    def one(dim, parts):
        steps = jax.random.uniform(jax.random.fold_in(jax.random.fold_in(key, 6), dim), (parts,), jnp.float32, least / len(cuts), top_value / len(cuts))
        return jnp.repeat(jnp.exp(steps), extent[dim] // parts).reshape((-1,) + (1,) * (len(extent) - dim - 1))

    factor_of = one(*cuts[0])
    for cut in cuts[1:]:
        factor_of = factor_of * one(*cut)
    return factor_of


def normal_values(key, dims, scale, limit, cuts=(), kind=jnp.bfloat16):
    values = jax.random.normal(key, dims, jnp.float32) * scale
    if len(cuts) > 0:
        values = level_of(key, dims, cuts, -0.22, 0.18) * values
    return jnp.clip(values, min=-limit, max=limit).astype(kind)


def setup_inputs(seed: int = 0) -> dict:
    keys = jax.random.split(jax.random.key(seed), 6)
    velocity = normal_values(keys[0], (WIN, PATCHES, NT), 1.0, 6.0, ((1, 512),))
    radiation_modes = normal_values(keys[1], (PATCHES, RMAX), (PATCHES // 4) ** -0.5, 0.03125, ((0, 128), (1, 4)))
    resistance = draw_resistance(jax.random.fold_in(keys[5], 71), 0)
    mode_ranks = draw_mode_ranks(jax.random.fold_in(keys[5], 71), 0)
    freq_table = jax.random.permutation(keys[4], F).astype(jnp.int32)
    return {"velocity": velocity, "radiation_modes": radiation_modes, "resistance": resistance, "mode_ranks": mode_ranks, "freq_table": freq_table}


def make_table(freq_table):
    times = jnp.arange(NT, dtype=jnp.int32)
    phases = times[:, None] * freq_table[None, :].astype(jnp.int32) % NT
    angles = phases.astype(jnp.float32) * (2.0 * math.pi / NT)
    norming = 1.0 / math.sqrt(NT)
    table = jnp.stack([jnp.cos(angles), -jnp.sin(angles)], axis=1) * norming
    return table.astype(jnp.bfloat16)

def reference(velocity, radiation_modes, resistance, mode_ranks, freq_table):
    table_wide = make_table(freq_table).astype(jnp.float32)
    modes_wide = radiation_modes.astype(jnp.float32)
    rank_mask = (jnp.arange(RMAX, dtype=jnp.int32)[:, None] < mode_ranks[None, :]).astype(jnp.float32)
    rank_mask = rank_mask[:, None, :, None]
    results = []
    for window in range(WIN):
        spectra = jnp.einsum('pt,tcf->pcf', velocity[window].astype(jnp.float32), table_wide).astype(jnp.bfloat16)
        coefficients = jnp.einsum('pr,pcf->rcf', modes_wide, spectra.astype(jnp.float32))
        coefficients = coefficients.reshape(RMAX, 2, NBANDS, FPB) * rank_mask
        forcing = jnp.einsum('bij,jcbf->icbf', resistance, coefficients, precision=lax.Precision.HIGHEST)
        forcing = (2.0 * forcing * rank_mask).astype(jnp.bfloat16).reshape(RMAX, 2, F)
        surface_force = jnp.einsum('pr,rcf->pcf', modes_wide, forcing.astype(jnp.float32)).astype(jnp.bfloat16)
        history = jnp.einsum('pcf,tcf->pt', surface_force.astype(jnp.float32), table_wide)
        results.append(history.astype(jnp.bfloat16))
    return jnp.stack(results, axis=0)
```

```python
import functools
import math

import jax
import jax.numpy as jnp
from jax import lax
from jax.experimental import pallas as pl
from jax.experimental.pallas import tpu as pltpu
from jax.sharding import Mesh
from jax.sharding import PartitionSpec as P

Z, Y, CORE, MODE = "band_0", "band_1", "band_2", "mode"
F32, BF16 = jnp.float32, jnp.bfloat16
LANES = 128
VMEM = 24 * 1024 * 1024


def call(kernel, out_shape, flops, **options):
    whole = pl.BlockSpec(memory_space=pltpu.VMEM)
    return pl.pallas_call(
        kernel,
        out_shape=out_shape,
        compiler_params=pltpu.CompilerParams(vmem_limit_bytes=VMEM),
        cost_estimate=pl.CostEstimate(flops=flops, bytes_accessed=4 << 20, transcendentals=0),
        **options,
    )


def dot(a, b):
    return jnp.dot(a, b, preferred_element_type=F32)


def dot_t(a, b):
    return lax.dot_general(a, b, (((1,), (1,)), ((), ())), preferred_element_type=F32)


def spectra_kernel(steps, freq_ref, part_ref, velocity_ref, table_ref, spectra_ref):
    rows = freq_ref.shape[0]
    freq = freq_ref[...]
    part = part_ref[...]
    low = lax.broadcasted_iota(jnp.int32, (rows, LANES), 1)
    turn = 2.0 * math.pi / steps
    phase = (low * freq + part * (steps // 4)) & (steps - 1)
    angle = phase.astype(F32) * turn
    cos_low = jnp.cos(angle) * (1.0 / math.sqrt(steps))
    sin_low = jnp.sin(angle) * (1.0 / math.sqrt(steps))
    for high in range(steps // LANES):
        coarse = ((high * LANES * freq) & (steps - 1)).astype(F32) * turn
        piece = cos_low * jnp.cos(coarse) - sin_low * jnp.sin(coarse)
        table_ref[:, high * LANES : (high + 1) * LANES] = piece.astype(BF16)
    spectra_ref[...] = dot_t(table_ref[...], velocity_ref[...]).astype(BF16)


def make_spectra(freq, part, velocity):
    rows = freq.shape[0]
    patches, steps = velocity.shape
    tile = rows // 4
    return call(
        functools.partial(spectra_kernel, steps),
        (
            jax.ShapeDtypeStruct((rows, steps), BF16),
            jax.ShapeDtypeStruct((rows, patches), BF16),
        ),
        2 * rows * patches * steps,
        grid=(4,),
        in_specs=[
            pl.BlockSpec((tile, 1), lambda i: (i, 0)),
            pl.BlockSpec((tile, 1), lambda i: (i, 0)),
            pl.BlockSpec((patches, steps), lambda i: (0, 0)),
        ],
        out_specs=(
            pl.BlockSpec((tile, steps), lambda i: (i, 0)),
            pl.BlockSpec((tile, patches), lambda i: (i, 0)),
        ),
    )(freq, part, velocity)


def partial_kernel(spectra_ref, basis_ref, out_ref):
    width = basis_ref.shape[2]
    for k in range(basis_ref.shape[0]):
        out_ref[:, k * width : (k + 1) * width] = dot(spectra_ref[...], basis_ref[k]).astype(BF16)


def make_partial(spectra, basis, half):
    rows, patches = spectra.shape
    parts, _, width = basis.shape
    tile = rows // 4
    return call(
        partial_kernel,
        jax.ShapeDtypeStruct((rows // 2, parts * width), BF16),
        rows * patches * parts * width,
        grid=(2,),
        in_specs=[
            pl.BlockSpec((tile, patches), lambda i: (2 * half + i, 0)),
            pl.BlockSpec(basis.shape, lambda i: (0, 0, 0)),
        ],
        out_specs=pl.BlockSpec((tile, parts * width), lambda i: (i, 0)),
    )(spectra, basis)


def forcing_kernel(rank_ref, offset_ref, coef_ref, matrix_ref, out_ref):
    rank = rank_ref[0]
    total = coef_ref[0].astype(F32)
    for k in range(1, coef_ref.shape[0]):
        total = total + coef_ref[k].astype(F32)
    index = lax.broadcasted_iota(jnp.int32, total.shape, 1)
    total = jnp.where(index < rank, total, 0.0)
    forcing = dot(total.astype(BF16), matrix_ref[...].astype(BF16))
    index = lax.broadcasted_iota(jnp.int32, forcing.shape, 1) + offset_ref[0]
    out_ref[...] = jnp.where(index < rank, 2.0 * forcing, 0.0).astype(BF16)


def make_forcing(rank, offset, coef, matrix):
    rows = coef.shape[1]
    smem = pl.BlockSpec(memory_space=pltpu.SMEM)
    vmem = pl.BlockSpec(memory_space=pltpu.VMEM)
    return call(
        forcing_kernel,
        jax.ShapeDtypeStruct((rows, matrix.shape[1]), BF16),
        2 * rows * matrix.shape[0] * matrix.shape[1],
        in_specs=[smem, smem, vmem, vmem],
        out_specs=vmem,
    )(rank, offset, coef, matrix)


def history_kernel(basis_ref, forcing_ref, table_ref, *rest):
    out_ref = rest[-1]
    total = dot_t(basis_ref[0], forcing_ref[0])
    for k in range(1, basis_ref.shape[0]):
        total = total + dot_t(basis_ref[k], forcing_ref[k])
    history = dot(total.astype(BF16), table_ref[...])
    if len(rest) > 1:
        history = history + rest[0][...]
    out_ref[...] = history.astype(out_ref.dtype)


def make_history(basis, forcing, table, half, before, dtype):
    parts, patches, width = basis.shape
    rows = forcing.shape[1]
    steps = table.shape[1]
    more = [] if before is None else [before]
    whole = pl.BlockSpec(memory_space=pltpu.VMEM)
    return call(
        history_kernel,
        jax.ShapeDtypeStruct((patches, steps), dtype),
        2 * rows * patches * (steps + parts * width),
        grid=(1,),
        in_specs=[
            pl.BlockSpec(basis.shape, lambda i: (0, 0, 0)),
            pl.BlockSpec(forcing.shape, lambda i: (0, 0, 0)),
            pl.BlockSpec((rows, steps), lambda i: (half, 0)),
        ]
        + [pl.BlockSpec(x.shape, lambda i: (0, 0)) for x in more],
        out_specs=pl.BlockSpec((patches, steps), lambda i: (0, 0)),
    )(basis, forcing, table, *more)


def exchange(value, axis):
    return lax.all_to_all(value, axis, split_axis=0, concat_axis=0, tiled=True)


def spread(value, axis):
    return exchange(jnp.broadcast_to(value, (lax.axis_size(axis), *value.shape)), axis)


def reduced(value, axis):
    count = lax.axis_size(axis)
    parts = exchange(value.reshape(count, value.shape[0] // count, value.shape[1]), axis)
    return jnp.sum(parts.astype(F32), axis=0).astype(BF16)


def swap_cores(value):
    return lax.ppermute(value, CORE, [(0, 1), (1, 0)])


def table_rows(freq_table):
    sizes = [lax.axis_size(a) for a in (Z, Y, CORE)]
    freq = freq_table.reshape(*sizes, -1).transpose(2, 1, 0, 3)
    freq = jnp.broadcast_to(freq[:, :, :, None, :], (*freq.shape[:3], 2, freq.shape[3]))
    part = lax.broadcasted_iota(jnp.int32, freq.shape, 3)
    here = lax.axis_index(CORE)
    freq = jnp.where(here == 0, freq[::-1], freq)
    return freq.reshape(-1, 1), part.reshape(-1, 1)


def per_device(velocity, radiation_modes, resistance, mode_ranks, freq_table):
    mode_count = lax.axis_size(MODE)
    width = radiation_modes.shape[1]
    basis = exchange(radiation_modes.reshape(mode_count, -1, width), MODE)
    freq, part = table_rows(freq_table)
    table, spectra = make_spectra(freq, part, velocity[0])
    received = swap_cores(make_partial(spectra, basis, 0))
    own = make_partial(spectra, basis, 1)
    coef = (own.astype(F32) + received.astype(F32)).astype(BF16)
    coef = reduced(coef, Y)
    coef = reduced(coef, Z)
    coef = spread(coef, MODE)
    offset = (lax.axis_index(MODE) * width).reshape(1)
    forcing = make_forcing(mode_ranks, offset, coef, resistance[0])
    forcing = spread(forcing, Z)
    forcing = spread(forcing.reshape(-1, width), (MODE, Y))
    forcing = forcing.reshape(mode_count, -1, width)
    received = swap_cores(forcing)
    history = make_history(basis, forcing, table, 1, None, F32)
    history = make_history(basis, received, table, 0, history, BF16)
    return history[None]


def solution(mesh):
    torus = Mesh(mesh.devices.reshape(16, 4, 2, mesh.shape["mode"]), (Z, Y, CORE, MODE))
    bands = (Z, Y, CORE)
    patches = (Z, Y, CORE, MODE)
    in_specs = (P(None, patches, None), P(bands, MODE), P(bands, None, MODE), P(bands), P())
    return jax.shard_map(
        per_device, mesh=torus, in_specs=in_specs, out_specs=P(None, patches, None), check_vma=False
    )
```

```python
import functools
import math

import jax
import jax.numpy as jnp
from jax import lax
from jax.experimental import pallas as pl
from jax.experimental.pallas import tpu as pltpu
from jax.sharding import Mesh
from jax.sharding import PartitionSpec as P

Z, Y, CORE, MODE = "band_0", "band_1", "band_2", "mode"
F32, BF16, I32 = jnp.float32, jnp.bfloat16, jnp.int32
LANES = 128
VMEM_BYTES = 24 * 1024 * 1024
SMEM = pl.BlockSpec(memory_space=pltpu.SMEM)
WHOLE = pl.BlockSpec(memory_space=pltpu.VMEM)


def shape(dims, dtype):
    return jax.ShapeDtypeStruct(tuple(dims), dtype)


def call(kernel, out_shape, flops, **options):
    return pl.pallas_call(
        kernel,
        out_shape=out_shape,
        compiler_params=pltpu.CompilerParams(vmem_limit_bytes=VMEM_BYTES),
        cost_estimate=pl.CostEstimate(flops=flops, bytes_accessed=1 << 20, transcendentals=0),
        **options,
    )


def dot(a, b):
    return jnp.dot(a, b, preferred_element_type=F32)


def dot_t(a, b):
    return lax.dot_general(a, b, (((1,), (1,)), ((), ())), preferred_element_type=F32)


def sin_cos(phase, steps):
    quadrant = (phase + steps // 8) >> (int(math.log2(steps)) - 2)
    x = (phase - quadrant * (steps // 4)).astype(F32) * (2.0 * math.pi / steps)
    y = x * x
    sin = x * (1.0 + y * (-1 / 6 + y * (1 / 120 + y * (-1 / 5040 + y * (1 / 362880)))))
    cos = 1.0 + y * (-1 / 2 + y * (1 / 24 + y * (-1 / 720 + y * (1 / 40320 - y * (1 / 3628800)))))
    odd = (quadrant & 1) == 1
    sign_sin = jnp.where((quadrant & 2) == 2, -1.0, 1.0)
    sign_cos = jnp.where(((quadrant + 1) & 2) == 2, -1.0, 1.0)
    return jnp.where(odd, cos, sin) * sign_sin, jnp.where(odd, sin, cos) * sign_cos


def cos_eighth(k):
    size = jnp.where((k & 1) == 1, math.sqrt(0.5), jnp.where((k & 2) == 2, 0.0, 1.0))
    return jnp.where(((k + 1) & 4) == 4, -size, size)


def spectra_kernel(
    z_count, y_count, slots, core_ref, freq_ref, velocity_ref, matrix_ref, table_ref, out_ref, rounded_ref
):
    rows, steps = table_ref.shape
    all_slots = freq_ref.shape[1]
    row = lax.broadcasted_iota(I32, (rows, all_slots), 0)
    source = (row // (2 * slots) * y_count + pl.program_id(0)) * (2 * slots)
    source = source + core_ref[0] * slots + (row & (slots - 1))
    lane = lax.broadcasted_iota(I32, (rows, all_slots), 1)
    freq = jnp.where(lane == source, freq_ref[...].astype(F32), 0.0)
    freq = jnp.sum(freq, axis=1, keepdims=True).astype(I32)
    freq = jnp.broadcast_to(freq, (rows, LANES))
    row = lax.broadcasted_iota(I32, (rows, LANES), 0)
    low = lax.broadcasted_iota(I32, (rows, LANES), 1)
    imaginary = (row // slots) & 1
    phase = (low * freq + imaginary * (steps // 4)) & (steps - 1)
    sin_low, cos_low = sin_cos(phase, steps)
    norming = 1.0 / math.sqrt(steps)
    sin_low, cos_low = sin_low * norming, cos_low * norming
    for high in range(steps // LANES):
        eighth = (freq * (high * LANES * 8 // steps)) & 7
        piece = cos_low * cos_eighth(eighth) - sin_low * cos_eighth((eighth + 6) & 7)
        table_ref[:, high * LANES : (high + 1) * LANES] = piece.astype(BF16)
    out_ref[...] = dot_t(table_ref[...], velocity_ref[...]).astype(BF16)
    rounded_ref[...] = matrix_ref[...].astype(BF16)


def make_spectra(core, freq_table, velocity, matrix):
    z_count, y_count = lax.axis_size(Z), lax.axis_size(Y)
    all_slots = freq_table.shape[0]
    slots = all_slots // (z_count * y_count * lax.axis_size(CORE))
    patches, steps = velocity.shape
    assert 8 * LANES == steps and slots & (slots - 1) == 0
    tile = z_count * 2 * slots
    rows = tile * y_count
    depth, width = matrix.shape
    return call(
        functools.partial(spectra_kernel, z_count, y_count, slots),
        (shape((rows, steps), BF16), shape((rows, patches), BF16), shape((depth, width), BF16)),
        2 * rows * patches * steps,
        grid=(y_count,),
        in_specs=[
            SMEM,
            pl.BlockSpec((1, all_slots), lambda i: (0, 0)),
            pl.BlockSpec((patches, steps), lambda i: (0, 0)),
            pl.BlockSpec((depth // y_count, width), lambda i: (i, 0)),
        ],
        out_specs=(
            pl.BlockSpec((tile, steps), lambda i: (i, 0)),
            pl.BlockSpec((tile, patches), lambda i: (i, 0)),
            pl.BlockSpec((depth // y_count, width), lambda i: (i, 0)),
        ),
    )(core, freq_table.reshape(1, -1), velocity, matrix)


def other_kernel(table_ref, velocity_ref, out_ref):
    out_ref[...] = dot_t(table_ref[...], velocity_ref[...]).astype(BF16)


def other_spectra(table, velocity):
    rows, patches = table.shape[0], velocity.shape[0]
    return call(
        other_kernel,
        shape((rows, patches), BF16),
        2 * rows * velocity.size,
        in_specs=[WHOLE, WHOLE],
        out_specs=WHOLE,
    )(table, velocity)


def partial_kernel(spectra_ref, basis_ref, *rest):
    out_ref = rest[-1]
    value = dot(spectra_ref[...], basis_ref[0])
    if len(rest) > 1:
        value = value + rest[0][0]
    out_ref[0] = value.astype(out_ref.dtype)


def make_partial(spectra, basis, before, dtype):
    rows, patches = spectra.shape
    parts, _, width = basis.shape
    more = [] if before is None else [before]
    return call(
        partial_kernel,
        shape((parts, rows, width), dtype),
        2 * rows * patches * parts * width,
        grid=(parts,),
        in_specs=[
            pl.BlockSpec((rows, patches), lambda i: (0, 0)),
            pl.BlockSpec((1, patches, width), lambda i: (i, 0, 0)),
        ]
        + [pl.BlockSpec((1, rows, width), lambda i: (i, 0, 0)) for _ in more],
        out_specs=pl.BlockSpec((1, rows, width), lambda i: (i, 0, 0)),
    )(spectra, basis, *more)


def added(parts_ref):
    total = parts_ref[0].astype(F32)
    for k in range(1, parts_ref.shape[0]):
        total = total + parts_ref[k].astype(F32)
    return total


def sum_kernel(parts_ref, out_ref):
    out_ref[...] = added(parts_ref).astype(BF16)


def summed(parts):
    return call(
        sum_kernel, shape(parts.shape[1:], BF16), parts.size, in_specs=[WHOLE], out_specs=WHOLE
    )(parts)


def kept(value, rank_ref, offset_ref):
    index = lax.broadcasted_iota(I32, value.shape, 1) + offset_ref[0]
    return jnp.where(index < rank_ref[0], value, 0.0)


def coefficients_kernel(rank_ref, offset_ref, parts_ref, out_ref):
    value = kept(added(parts_ref), rank_ref, offset_ref).astype(BF16)
    out_ref[...] = jnp.broadcast_to(value, out_ref.shape)


def make_coefficients(rank, offset, parts, copies):
    return call(
        coefficients_kernel,
        shape((copies, *parts.shape[1:]), BF16),
        parts.size,
        in_specs=[SMEM, SMEM, WHOLE],
        out_specs=WHOLE,
    )(rank, offset, parts)


def forcing_kernel(rank_ref, offset_ref, coef_ref, matrix_ref, out_ref):
    width = coef_ref.shape[2]
    total = dot(coef_ref[0], matrix_ref[:width])
    for k in range(1, coef_ref.shape[0]):
        total = total + dot(coef_ref[k], matrix_ref[k * width : (k + 1) * width])
    value = kept(2.0 * total, rank_ref, offset_ref).astype(BF16)
    out_ref[...] = jnp.broadcast_to(value, out_ref.shape)


def make_forcing(rank, offset, coef, matrix, copies):
    rows = coef.shape[1]
    return call(
        forcing_kernel,
        shape((copies, rows, matrix.shape[1]), BF16),
        2 * rows * matrix.size,
        in_specs=[SMEM, SMEM, WHOLE, WHOLE],
        out_specs=WHOLE,
    )(rank, offset, coef, matrix)


def history_kernel(basis_ref, forcing_ref, table_ref, out_ref):
    total = dot_t(basis_ref[0], forcing_ref[0])
    for k in range(1, basis_ref.shape[0]):
        total = total + dot_t(basis_ref[k], forcing_ref[k])
    out_ref[...] = dot(total.astype(BF16), table_ref[...]).astype(out_ref.dtype)


def make_history(basis, forcing, table, dtype):
    parts, patches, width = basis.shape
    rows, steps = table.shape
    return call(
        history_kernel,
        shape((patches, steps), dtype),
        2 * rows * patches * (steps + parts * width),
        in_specs=[WHOLE, WHOLE, WHOLE],
        out_specs=WHOLE,
    )(basis, forcing, table)


def exchange(value, axis):
    return lax.all_to_all(value, axis, split_axis=0, concat_axis=0, tiled=True)


def swap_cores(value):
    return lax.ppermute(value, CORE, [(0, 1), (1, 0)])


def per_device(velocity, radiation_modes, resistance, mode_ranks, freq_table):
    modes, ys, zs = lax.axis_size(MODE), lax.axis_size(Y), lax.axis_size(Z)
    width = radiation_modes.shape[1]
    core = lax.axis_index(CORE).reshape(1)
    offset = (lax.axis_index(MODE) * width).reshape(1)
    basis = exchange(radiation_modes.reshape(modes, -1, width), MODE)
    velocity_other = swap_cores(velocity[0])
    table, spectra, matrix = make_spectra(core, freq_table, velocity[0], resistance[0])
    spectra_other = other_spectra(table, velocity_other)
    basis, spectra, spectra_other = lax.optimization_barrier((basis, spectra, spectra_other))
    basis_other = swap_cores(basis)
    coef = make_partial(spectra, basis, None, F32)
    coef = make_partial(spectra_other, basis_other, coef, BF16)
    coef = summed(exchange(coef.reshape(modes * ys, -1, width), (MODE, Y)))
    coef = exchange(coef.reshape(zs, -1, width), Z)
    coef = exchange(make_coefficients(mode_ranks, offset, coef, modes), MODE)
    forcing = exchange(make_forcing(mode_ranks, offset, coef, matrix, zs), Z)
    forcing = forcing.reshape(-1, width)
    forcing = exchange(jnp.broadcast_to(forcing, (modes * ys, *forcing.shape)), (MODE, Y))
    forcing = forcing.reshape(modes, -1, width)
    sent = make_history(basis_other, forcing, table, BF16)
    received = swap_cores(sent)
    history = make_history(basis, forcing, table, F32)
    return (history + received.astype(F32)).astype(BF16)[None]


def solution(mesh):
    torus = Mesh(mesh.devices.reshape(16, 4, 2, mesh.shape["mode"]), (Z, Y, CORE, MODE))
    bands = (Z, Y, CORE)
    patches = (Z, Y, CORE, MODE)
    in_specs = (P(None, patches, None), P(bands, MODE), P(bands, None, MODE), P(bands), P())
    return jax.shard_map(
        per_device, mesh=torus, in_specs=in_specs, out_specs=P(None, patches, None), check_vma=False
    )
```

```python
import functools
import math

import jax
import jax.numpy as jnp
from jax import lax
from jax.experimental import pallas as pl
from jax.experimental.pallas import tpu as pltpu
from jax.sharding import Mesh
from jax.sharding import PartitionSpec as P

Z, Y, CORE, MODE = "band_0", "band_1", "band_2", "mode"
F32, BF16, I32 = jnp.float32, jnp.bfloat16, jnp.int32
LANES = 128
VMEM_BYTES = 24 * 1024 * 1024
SMEM = pl.BlockSpec(memory_space=pltpu.SMEM)
WHOLE = pl.BlockSpec(memory_space=pltpu.VMEM)


def shape(dims, dtype):
    return jax.ShapeDtypeStruct(tuple(dims), dtype)


def call(kernel, out_shape, flops, bytes_accessed=1 << 20, **options):
    return pl.pallas_call(
        kernel,
        out_shape=out_shape,
        compiler_params=pltpu.CompilerParams(vmem_limit_bytes=VMEM_BYTES),
        cost_estimate=pl.CostEstimate(
            flops=flops, bytes_accessed=bytes_accessed, transcendentals=0
        ),
        **options,
    )


def dot(a, b):
    return jnp.dot(a, b, preferred_element_type=F32)


def dot_t(a, b):
    return lax.dot_general(a, b, (((1,), (1,)), ((), ())), preferred_element_type=F32)


def sin_cos(phase, steps):
    quadrant = (phase + steps // 8) >> (int(math.log2(steps)) - 2)
    x = (phase - quadrant * (steps // 4)).astype(F32) * (2.0 * math.pi / steps)
    y = x * x
    sin = x * (1.0 + y * (-1 / 6 + y * (1 / 120 + y * (-1 / 5040 + y * (1 / 362880)))))
    cos = 1.0 + y * (-1 / 2 + y * (1 / 24 + y * (-1 / 720 + y * (1 / 40320 - y * (1 / 3628800)))))
    odd = (quadrant & 1) == 1
    sign_sin = jnp.where((quadrant & 2) == 2, -1.0, 1.0)
    sign_cos = jnp.where(((quadrant + 1) & 2) == 2, -1.0, 1.0)
    return jnp.where(odd, cos, sin) * sign_sin, jnp.where(odd, sin, cos) * sign_cos


def cos_eighth(k):
    size = jnp.where((k & 1) == 1, math.sqrt(0.5), jnp.where((k & 2) == 2, 0.0, 1.0))
    return jnp.where(((k + 1) & 4) == 4, -size, size)


def make_table(slots, y_count, core, freq_in, table_ref):
    all_rows, steps = table_ref.shape
    all_slots = freq_in.shape[1]
    rows = all_rows // y_count
    cores = 2 * all_slots // all_rows
    shift = int(math.log2(slots))
    turns = steps // LANES
    norming = 1.0 / math.sqrt(steps)
    row = lax.broadcasted_iota(I32, (rows, 1), 0)
    first = (row >> (shift + 1)) * (y_count * cores * slots) + (row & (slots - 1)) + core * slots
    lane = lax.broadcasted_iota(I32, (rows, all_slots), 1)
    low = lax.broadcasted_iota(I32, (rows, LANES), 1)
    quarter = ((row >> shift) & 1) * (steps // 4)
    for y in range(y_count):
        here = slice(y * rows, (y + 1) * rows)
        freq = jnp.where(lane == first + y * cores * slots, freq_in[...].astype(F32), 0.0)
        freq = jnp.sum(freq, axis=1, keepdims=True).astype(I32)
        freq = jnp.broadcast_to(freq, (rows, LANES))
        sin, cos = sin_cos((low * freq + quarter) & (steps - 1), steps)
        sin, cos = sin * norming, cos * norming
        turn_cos, turn_sin = cos_eighth(freq & 7), cos_eighth((freq + 6) & 7)
        half_turn = jnp.where((freq & 1) == 1, -1.0, 1.0)
        for k in range(turns // 2):
            table_ref[here, k * LANES : (k + 1) * LANES] = cos.astype(BF16)
            far = k + turns // 2
            table_ref[here, far * LANES : (far + 1) * LANES] = (cos * half_turn).astype(BF16)
            cos, sin = cos * turn_cos - sin * turn_sin, sin * turn_cos + cos * turn_sin


def sent_kernel(
    slots, y_count, place_ref, freq_ref, velocity_ref, out_ref, freq_in, velocity_in, table, sems
):
    copies = [
        pltpu.make_async_copy(freq_ref, freq_in, sems.at[0]),
        pltpu.make_async_copy(velocity_ref, velocity_in, sems.at[1]),
    ]
    for copy in copies:
        copy.start()
    copies[0].wait()
    make_table(slots, y_count, 1 - place_ref[0], freq_in, table)
    copies[1].wait()
    out_ref[...] = dot_t(table[...], velocity_in[...]).astype(BF16)


def own_kernel(
    slots, y_count, place_ref, rank_ref, freq_ref, velocity_ref, matrix_ref,
    table_ref, out_ref, rounded_ref, limits_ref, matrix_in, sem,
):
    copy = pltpu.make_async_copy(matrix_ref, matrix_in, sem)
    copy.start()
    limits_ref[0] = rank_ref[0]
    limits_ref[1] = place_ref[1] * matrix_ref.shape[1]
    make_table(slots, y_count, place_ref[0], freq_ref, table_ref)
    out_ref[...] = dot_t(table_ref[...], velocity_ref[...]).astype(BF16)
    copy.wait()
    rounded_ref[...] = matrix_in[...].astype(BF16)


def in_hbm(value):
    return pltpu.with_memory_space_constraint(value, pltpu.HBM)


def make_spectra(place, rank, freq_table, velocity, matrix):
    y_count, cores = lax.axis_size(Y), lax.axis_size(CORE)
    all_slots = freq_table.shape[0]
    slots = all_slots // (lax.axis_size(Z) * y_count * cores)
    patches, steps = velocity.shape
    assert 8 * LANES == steps and slots & (slots - 1) == 0 and cores == 2
    rows = 2 * all_slots // cores
    hbm = pl.BlockSpec(memory_space=pltpu.HBM)
    table, spectra = shape((rows, steps), BF16), shape((rows, patches), BF16)
    sent, freq, velocity = call(
        functools.partial(sent_kernel, slots, y_count),
        (spectra, shape((1, all_slots), I32), shape(velocity.shape, BF16)),
        1,
        1,
        in_specs=[SMEM, hbm, hbm],
        out_specs=(WHOLE, WHOLE, WHOLE),
        scratch_shapes=[pltpu.VMEM((rows, steps), BF16), pltpu.SemaphoreType.DMA((2,))],
    )(place, in_hbm(freq_table.reshape(1, -1)), in_hbm(velocity))
    own = call(
        functools.partial(own_kernel, slots, y_count),
        (table, spectra, shape(matrix.shape, BF16), shape((2,), I32)),
        1,
        1,
        in_specs=[SMEM, SMEM, WHOLE, WHOLE, hbm],
        out_specs=(WHOLE, WHOLE, WHOLE, SMEM),
        scratch_shapes=[pltpu.VMEM(matrix.shape, F32), pltpu.SemaphoreType.DMA],
    )(place, rank, freq, velocity, in_hbm(matrix))
    return sent, *own


def partial_kernel(spectra_ref, basis_ref, before_ref, out_ref):
    for k in range(basis_ref.shape[0]):
        out_ref[k] = (dot(spectra_ref[...], basis_ref[k]) + before_ref[k]).astype(BF16)


def make_partial(spectra, basis, before):
    return call(
        partial_kernel,
        shape(before.shape, BF16),
        2 * before.size * spectra.shape[1],
        in_specs=[WHOLE] * 3,
        out_specs=WHOLE,
    )(spectra, basis, before)


def first_kernel(spectra_ref, basis_ref, out_ref):
    for k in range(basis_ref.shape[0]):
        out_ref[k] = dot(spectra_ref[...], basis_ref[k])


def first_partial(spectra, basis):
    rows, patches = spectra.shape
    parts, _, width = basis.shape
    return call(
        first_kernel,
        shape((parts, rows, width), F32),
        2 * rows * patches * parts * width,
        in_specs=[WHOLE, WHOLE],
        out_specs=WHOLE,
    )(spectra, basis)


def added(parts_ref):
    total = parts_ref[0].astype(F32)
    for k in range(1, parts_ref.shape[0]):
        total = total + parts_ref[k].astype(F32)
    return total


def sum_kernel(parts_ref, out_ref):
    out_ref[...] = added(parts_ref).astype(BF16)


def summed(parts):
    return call(
        sum_kernel, shape(parts.shape[1:], BF16), parts.size, in_specs=[WHOLE], out_specs=WHOLE
    )(parts)


def kept(value, limits_ref):
    index = lax.broadcasted_iota(I32, value.shape, 1) + limits_ref[1]
    return jnp.where(index < limits_ref[0], value, 0.0)


def coefficients_kernel(limits_ref, parts_ref, out_ref):
    value = kept(added(parts_ref), limits_ref).astype(BF16)
    out_ref[...] = jnp.broadcast_to(value, out_ref.shape)


def make_coefficients(limits, parts, copies):
    return call(
        coefficients_kernel,
        shape((copies, *parts.shape[1:]), BF16),
        parts.size,
        in_specs=[SMEM, WHOLE],
        out_specs=WHOLE,
    )(limits, parts)


def forcing_kernel(limits_ref, coef_ref, matrix_ref, out_ref):
    width = coef_ref.shape[2]
    total = dot(coef_ref[0], matrix_ref[:width])
    for k in range(1, coef_ref.shape[0]):
        total = total + dot(coef_ref[k], matrix_ref[k * width : (k + 1) * width])
    value = kept(2.0 * total, limits_ref).astype(BF16)
    out_ref[...] = jnp.broadcast_to(value, out_ref.shape)


def make_forcing(limits, coef, matrix, copies):
    rows = coef.shape[1]
    return call(
        forcing_kernel,
        shape((copies, rows, matrix.shape[1]), BF16),
        2 * rows * matrix.size,
        in_specs=[SMEM, WHOLE, WHOLE],
        out_specs=WHOLE,
    )(limits, coef, matrix)


def history_kernel(basis_ref, forcing_ref, table_ref, *rest):
    out_ref = rest[-1]
    total = dot_t(basis_ref[0], forcing_ref[0])
    for k in range(1, basis_ref.shape[0]):
        total = total + dot_t(basis_ref[k], forcing_ref[k])
    out_ref[...] = dot(total.astype(BF16), table_ref[...]).astype(out_ref.dtype)


def make_history(basis, forcing, table, dtype):
    parts, patches, width = basis.shape
    rows = forcing.shape[1]
    steps = table.shape[1]
    return call(
        history_kernel,
        shape((patches, steps), dtype),
        2 * rows * patches * (steps + parts * width),
        grid=(1,),
        in_specs=[
            pl.BlockSpec(basis.shape, lambda i: (0, 0, 0)),
            pl.BlockSpec(forcing.shape, lambda i: (0, 0, 0)),
            pl.BlockSpec((rows, steps), lambda i: (0, 0)),
        ],
        out_specs=pl.BlockSpec((patches, steps), lambda i: (0, 0)),
    )(basis, forcing, table)


def exchange(value, axis):
    return lax.all_to_all(value, axis, split_axis=0, concat_axis=0, tiled=True)


def swap_cores(value):
    return lax.ppermute(value, CORE, [(0, 1), (1, 0)])


def per_device(velocity, radiation_modes, resistance, mode_ranks, freq_table):
    modes, ys, zs = lax.axis_size(MODE), lax.axis_size(Y), lax.axis_size(Z)
    width = radiation_modes.shape[1]
    place = jnp.stack([lax.axis_index(CORE), lax.axis_index(MODE)])
    basis = exchange(radiation_modes.reshape(modes, -1, width), MODE)
    sent, table, spectra, matrix, limits = make_spectra(
        place, mode_ranks, freq_table, velocity[0], resistance[0]
    )
    spectra_other = swap_cores(sent)
    basis, spectra, spectra_other = lax.optimization_barrier((basis, spectra, spectra_other))
    basis_other = swap_cores(basis)
    coef = first_partial(spectra, basis)
    coef = make_partial(spectra_other, basis_other, coef)
    coef = summed(exchange(coef.reshape(modes * ys, -1, width), (MODE, Y)))
    coef = exchange(coef.reshape(zs, -1, width), Z)
    coef = exchange(make_coefficients(limits, coef, modes), MODE)
    forcing = exchange(make_forcing(limits, coef, matrix, zs), Z)
    forcing = forcing.reshape(-1, width)
    forcing = exchange(jnp.broadcast_to(forcing, (modes * ys, *forcing.shape)), (MODE, Y))
    forcing = forcing.reshape(modes, -1, width)
    received = swap_cores(make_history(basis_other, forcing, table, BF16))
    history = make_history(basis, forcing, table, F32)
    return (history + received.astype(F32)).astype(BF16)[None]


def solution(mesh):
    torus = Mesh(mesh.devices.reshape(16, 4, 2, mesh.shape["mode"]), (Z, Y, CORE, MODE))
    bands = (Z, Y, CORE)
    patches = (Z, Y, CORE, MODE)
    in_specs = (P(None, patches, None), P(bands, MODE), P(bands, None, MODE), P(bands), P())
    return jax.shard_map(
        per_device, mesh=torus, in_specs=in_specs, out_specs=P(None, patches, None), check_vma=False
    )
```

```python
import functools
import math

import jax
import jax.numpy as jnp
from jax import lax
from jax.experimental import pallas as pl
from jax.experimental.pallas import tpu as pltpu
from jax.sharding import Mesh
from jax.sharding import PartitionSpec as P

Z, Y, CORE, MODE = "band_0", "band_1", "band_2", "mode"
F32, BF16, I32 = jnp.float32, jnp.bfloat16, jnp.int32
LANES = 128
VMEM_BYTES = 24 * 1024 * 1024
SMEM = pl.BlockSpec(memory_space=pltpu.SMEM)
WHOLE = pl.BlockSpec(memory_space=pltpu.VMEM)


def shape(dims, dtype):
    return jax.ShapeDtypeStruct(tuple(dims), dtype)


def call(kernel, out_shape, flops, bytes_accessed=1 << 20, **options):
    return pl.pallas_call(
        kernel,
        out_shape=out_shape,
        compiler_params=pltpu.CompilerParams(vmem_limit_bytes=VMEM_BYTES),
        cost_estimate=pl.CostEstimate(
            flops=flops, bytes_accessed=bytes_accessed, transcendentals=0
        ),
        **options,
    )


def dot(a, b):
    return jnp.dot(a, b, preferred_element_type=F32)


def dot_t(a, b):
    return lax.dot_general(a, b, (((1,), (1,)), ((), ())), preferred_element_type=F32)


def sin_cos(phase, steps):
    quadrant = (phase + steps // 8) >> (int(math.log2(steps)) - 2)
    x = (phase - quadrant * (steps // 4)).astype(F32) * (2.0 * math.pi / steps)
    y = x * x
    sin = x * (1.0 + y * (-1 / 6 + y * (1 / 120 + y * (-1 / 5040 + y * (1 / 362880)))))
    cos = 1.0 + y * (-1 / 2 + y * (1 / 24 + y * (-1 / 720 + y * (1 / 40320 - y * (1 / 3628800)))))
    odd = (quadrant & 1) == 1
    sign_sin = jnp.where((quadrant & 2) == 2, -1.0, 1.0)
    sign_cos = jnp.where(((quadrant + 1) & 2) == 2, -1.0, 1.0)
    return jnp.where(odd, cos, sin) * sign_sin, jnp.where(odd, sin, cos) * sign_cos


def cos_eighth(k):
    size = jnp.where((k & 1) == 1, math.sqrt(0.5), jnp.where((k & 2) == 2, 0.0, 1.0))
    return jnp.where(((k + 1) & 4) == 4, -size, size)


def make_table(slots, y_count, core, freq_in, table_ref):
    all_rows, steps = table_ref.shape
    all_slots = freq_in.shape[1]
    rows = all_rows // y_count
    cores = 2 * all_slots // all_rows
    shift = int(math.log2(slots))
    turns = steps // LANES
    norming = 1.0 / math.sqrt(steps)
    row = lax.broadcasted_iota(I32, (rows, 1), 0)
    first = (row >> (shift + 1)) * (y_count * cores * slots) + (row & (slots - 1)) + core * slots
    lane = lax.broadcasted_iota(I32, (rows, all_slots), 1)
    low = lax.broadcasted_iota(I32, (rows, LANES), 1)
    quarter = ((row >> shift) & 1) * (steps // 4)
    for y in range(y_count):
        here = slice(y * rows, (y + 1) * rows)
        freq = jnp.where(lane == first + y * cores * slots, freq_in[...].astype(F32), 0.0)
        freq = jnp.sum(freq, axis=1, keepdims=True).astype(I32)
        freq = jnp.broadcast_to(freq, (rows, LANES))
        sin, cos = sin_cos((low * freq + quarter) & (steps - 1), steps)
        sin, cos = sin * norming, cos * norming
        turn_cos, turn_sin = cos_eighth(freq & 7), cos_eighth((freq + 6) & 7)
        half_turn = jnp.where((freq & 1) == 1, -1.0, 1.0)
        for k in range(turns // 2):
            table_ref[here, k * LANES : (k + 1) * LANES] = cos.astype(BF16)
            far = k + turns // 2
            table_ref[here, far * LANES : (far + 1) * LANES] = (cos * half_turn).astype(BF16)
            cos, sin = cos * turn_cos - sin * turn_sin, sin * turn_cos + cos * turn_sin


def sent_kernel(
    slots, y_count, place_ref, freq_ref, velocity_ref, matrix_ref,
    out_ref, freq_in, velocity_in, matrix_in, table, sems,
):
    copies = [
        pltpu.make_async_copy(freq_ref, freq_in, sems.at[0]),
        pltpu.make_async_copy(velocity_ref, velocity_in, sems.at[1]),
        pltpu.make_async_copy(matrix_ref, matrix_in, sems.at[2]),
    ]
    for copy in copies:
        copy.start()
    copies[0].wait()
    make_table(slots, y_count, 1 - place_ref[0], freq_in, table)
    copies[1].wait()
    out_ref[...] = dot_t(table[...], velocity_in[...]).astype(BF16)
    copies[2].wait()


def own_kernel(
    slots, y_count, place_ref, freq_ref, velocity_ref, matrix_ref, table_ref, out_ref, rounded_ref
):
    rounded_ref[...] = matrix_ref[...].astype(BF16)
    make_table(slots, y_count, place_ref[0], freq_ref, table_ref)
    out_ref[...] = dot_t(table_ref[...], velocity_ref[...]).astype(BF16)


def in_hbm(value):
    return pltpu.with_memory_space_constraint(value, pltpu.HBM)


def make_spectra(place, freq_table, velocity, matrix):
    y_count, cores = lax.axis_size(Y), lax.axis_size(CORE)
    all_slots = freq_table.shape[0]
    slots = all_slots // (lax.axis_size(Z) * y_count * cores)
    patches, steps = velocity.shape
    assert 8 * LANES == steps and slots & (slots - 1) == 0 and cores == 2
    rows = 2 * all_slots // cores
    hbm = pl.BlockSpec(memory_space=pltpu.HBM)
    table, spectra = shape((rows, steps), BF16), shape((rows, patches), BF16)
    sent, freq, velocity, matrix = call(
        functools.partial(sent_kernel, slots, y_count),
        (
            spectra,
            shape((1, all_slots), I32),
            shape(velocity.shape, BF16),
            shape(matrix.shape, F32),
        ),
        1,
        1,
        in_specs=[SMEM, hbm, hbm, hbm],
        out_specs=(WHOLE, WHOLE, WHOLE, WHOLE),
        scratch_shapes=[pltpu.VMEM((rows, steps), BF16), pltpu.SemaphoreType.DMA((3,))],
    )(place, in_hbm(freq_table.reshape(1, -1)), in_hbm(velocity), in_hbm(matrix))
    own = call(
        functools.partial(own_kernel, slots, y_count),
        (table, spectra, shape(matrix.shape, BF16)),
        1,
        1,
        in_specs=[SMEM, WHOLE, WHOLE, WHOLE],
        out_specs=(WHOLE, WHOLE, WHOLE),
    )(place, freq, velocity, matrix)
    return sent, *own


def partial_kernel(spectra_ref, basis_ref, before_ref, out_ref):
    for k in range(basis_ref.shape[0]):
        out_ref[k] = (dot(spectra_ref[...], basis_ref[k]) + before_ref[k]).astype(BF16)


def make_partial(spectra, basis, before):
    return call(
        partial_kernel,
        shape(before.shape, BF16),
        2 * before.size * spectra.shape[1],
        in_specs=[WHOLE] * 3,
        out_specs=WHOLE,
    )(spectra, basis, before)


def first_kernel(spectra_ref, basis_ref, out_ref):
    for k in range(basis_ref.shape[0]):
        out_ref[k] = dot(spectra_ref[...], basis_ref[k])


def first_partial(spectra, basis):
    rows, patches = spectra.shape
    parts, _, width = basis.shape
    return call(
        first_kernel,
        shape((parts, rows, width), F32),
        2 * rows * patches * parts * width,
        in_specs=[WHOLE, WHOLE],
        out_specs=WHOLE,
    )(spectra, basis)


def added(parts_ref):
    total = parts_ref[0].astype(F32)
    for k in range(1, parts_ref.shape[0]):
        total = total + parts_ref[k].astype(F32)
    return total


def sum_kernel(parts_ref, out_ref):
    out_ref[...] = added(parts_ref).astype(BF16)


def summed(parts):
    return call(
        sum_kernel, shape(parts.shape[1:], BF16), parts.size, in_specs=[WHOLE], out_specs=WHOLE
    )(parts)


def kept(value, limit_ref):
    index = lax.broadcasted_iota(I32, value.shape, 1)
    return jnp.where(index < limit_ref[:1, :1], value, 0.0)


def coefficients_kernel(limit_ref, parts_ref, out_ref):
    value = kept(added(parts_ref), limit_ref).astype(BF16)
    out_ref[...] = jnp.broadcast_to(value, out_ref.shape)


def make_coefficients(limit, parts, copies):
    return call(
        coefficients_kernel,
        shape((copies, *parts.shape[1:]), BF16),
        parts.size,
        in_specs=[WHOLE, WHOLE],
        out_specs=WHOLE,
    )(limit, parts)


def forcing_kernel(limit_ref, coef_ref, matrix_ref, out_ref):
    width = coef_ref.shape[2]
    total = dot(coef_ref[0], matrix_ref[:width])
    for k in range(1, coef_ref.shape[0]):
        total = total + dot(coef_ref[k], matrix_ref[k * width : (k + 1) * width])
    value = kept(2.0 * total, limit_ref).astype(BF16)
    out_ref[...] = jnp.broadcast_to(value, out_ref.shape)


def make_forcing(limit, coef, matrix, copies):
    rows = coef.shape[1]
    return call(
        forcing_kernel,
        shape((copies, rows, matrix.shape[1]), BF16),
        2 * rows * matrix.size,
        in_specs=[WHOLE, WHOLE, WHOLE],
        out_specs=WHOLE,
    )(limit, coef, matrix)


def history_kernel(basis_ref, forcing_ref, table_ref, *rest):
    out_ref = rest[-1]
    total = dot_t(basis_ref[0], forcing_ref[0])
    for k in range(1, basis_ref.shape[0]):
        total = total + dot_t(basis_ref[k], forcing_ref[k])
    out_ref[...] = dot(total.astype(BF16), table_ref[...]).astype(out_ref.dtype)


def make_history(basis, forcing, table, dtype):
    parts, patches, width = basis.shape
    rows = forcing.shape[1]
    steps = table.shape[1]
    return call(
        history_kernel,
        shape((patches, steps), dtype),
        2 * rows * patches * (steps + parts * width),
        grid=(1,),
        in_specs=[
            pl.BlockSpec(basis.shape, lambda i: (0, 0, 0)),
            pl.BlockSpec(forcing.shape, lambda i: (0, 0, 0)),
            pl.BlockSpec((rows, steps), lambda i: (0, 0)),
        ],
        out_specs=pl.BlockSpec((patches, steps), lambda i: (0, 0)),
    )(basis, forcing, table)


def exchange(value, axis):
    return lax.all_to_all(value, axis, split_axis=0, concat_axis=0, tiled=True)


def swap_cores(value):
    return lax.ppermute(value, CORE, [(0, 1), (1, 0)])


def per_device(velocity, radiation_modes, resistance, mode_ranks, freq_table):
    modes, ys, zs = lax.axis_size(MODE), lax.axis_size(Y), lax.axis_size(Z)
    width = radiation_modes.shape[1]
    place = lax.axis_index(CORE).reshape(1)
    basis = exchange(radiation_modes.reshape(modes, -1, width), MODE)
    sent, table, spectra, matrix = make_spectra(place, freq_table, velocity[0], resistance[0])
    spectra_other = swap_cores(sent)
    limit = jnp.broadcast_to(mode_ranks[0] - lax.axis_index(MODE) * width, (8, LANES))
    basis, spectra, spectra_other, limit = lax.optimization_barrier(
        (basis, spectra, spectra_other, limit)
    )
    basis_other = swap_cores(basis)
    coef = first_partial(spectra, basis)
    coef = make_partial(spectra_other, basis_other, coef)
    coef = summed(exchange(coef.reshape(modes * ys, -1, width), (MODE, Y)))
    coef = exchange(coef.reshape(zs, -1, width), Z)
    coef = exchange(make_coefficients(limit, coef, modes), MODE)
    forcing = exchange(make_forcing(limit, coef, matrix, zs), Z)
    forcing = forcing.reshape(-1, width)
    forcing = exchange(jnp.broadcast_to(forcing, (modes * ys, *forcing.shape)), (MODE, Y))
    forcing = forcing.reshape(modes, -1, width)
    received = swap_cores(make_history(basis_other, forcing, table, BF16))
    history = make_history(basis, forcing, table, F32)
    return (history + received.astype(F32)).astype(BF16)[None]


def solution(mesh):
    torus = Mesh(mesh.devices.reshape(16, 4, 2, mesh.shape["mode"]), (Z, Y, CORE, MODE))
    bands = (Z, Y, CORE)
    patches = (Z, Y, CORE, MODE)
    in_specs = (P(None, patches, None), P(bands, MODE), P(bands, None, MODE), P(bands), P())
    return jax.shard_map(
        per_device, mesh=torus, in_specs=in_specs, out_specs=P(None, patches, None), check_vma=False
    )
```

```python
import functools
import math

import jax
import jax.numpy as jnp
from jax import lax
from jax.experimental import pallas as pl
from jax.experimental.pallas import tpu as pltpu
from jax.sharding import Mesh
from jax.sharding import PartitionSpec as P

Z, Y, CORE, MODE = "band_0", "band_1", "band_2", "mode"
F32, BF16, I32 = jnp.float32, jnp.bfloat16, jnp.int32
LANES = 128
VMEM_BYTES = 24 * 1024 * 1024
SMEM = pl.BlockSpec(memory_space=pltpu.SMEM)
WHOLE = pl.BlockSpec(memory_space=pltpu.VMEM)


def shape(dims, dtype):
    return jax.ShapeDtypeStruct(tuple(dims), dtype)


def call(kernel, out_shape, flops, bytes_accessed=1 << 20, **options):
    return pl.pallas_call(
        kernel,
        out_shape=out_shape,
        compiler_params=pltpu.CompilerParams(vmem_limit_bytes=VMEM_BYTES),
        cost_estimate=pl.CostEstimate(
            flops=flops, bytes_accessed=bytes_accessed, transcendentals=0
        ),
        **options,
    )


def dot(a, b):
    return jnp.dot(a, b, preferred_element_type=F32)


def dot_t(a, b):
    return lax.dot_general(a, b, (((1,), (1,)), ((), ())), preferred_element_type=F32)


def sin_cos(phase, steps):
    quadrant = (phase + steps // 8) >> (int(math.log2(steps)) - 2)
    x = (phase - quadrant * (steps // 4)).astype(F32) * (2.0 * math.pi / steps)
    y = x * x
    sin = x * (1.0 + y * (-1 / 6 + y * (1 / 120 + y * (-1 / 5040 + y * (1 / 362880)))))
    cos = 1.0 + y * (-1 / 2 + y * (1 / 24 + y * (-1 / 720 + y * (1 / 40320 - y * (1 / 3628800)))))
    odd = (quadrant & 1) == 1
    sign_sin = jnp.where((quadrant & 2) == 2, -1.0, 1.0)
    sign_cos = jnp.where(((quadrant + 1) & 2) == 2, -1.0, 1.0)
    return jnp.where(odd, cos, sin) * sign_sin, jnp.where(odd, sin, cos) * sign_cos


def cos_eighth(k):
    size = jnp.where((k & 1) == 1, math.sqrt(0.5), jnp.where((k & 2) == 2, 0.0, 1.0))
    return jnp.where(((k + 1) & 4) == 4, -size, size)


def make_table(slots, y_count, core, freq_in, table_ref):
    all_rows, steps = table_ref.shape
    all_slots = freq_in.shape[1]
    rows = all_rows // y_count
    cores = 2 * all_slots // all_rows
    shift = int(math.log2(slots))
    turns = steps // LANES
    norming = 1.0 / math.sqrt(steps)
    row = lax.broadcasted_iota(I32, (rows, 1), 0)
    first = (row >> (shift + 1)) * (y_count * cores * slots) + (row & (slots - 1)) + core * slots
    lane = lax.broadcasted_iota(I32, (rows, all_slots), 1)
    low = lax.broadcasted_iota(I32, (rows, LANES), 1)
    quarter = ((row >> shift) & 1) * (steps // 4)
    for y in range(y_count):
        here = slice(y * rows, (y + 1) * rows)
        freq = jnp.where(lane == first + y * cores * slots, freq_in[...].astype(F32), 0.0)
        freq = jnp.sum(freq, axis=1, keepdims=True).astype(I32)
        freq = jnp.broadcast_to(freq, (rows, LANES))
        sin, cos = sin_cos((low * freq + quarter) & (steps - 1), steps)
        sin, cos = sin * norming, cos * norming
        turn_cos, turn_sin = cos_eighth(freq & 7), cos_eighth((freq + 6) & 7)
        half_turn = jnp.where((freq & 1) == 1, -1.0, 1.0)
        for k in range(turns // 2):
            table_ref[here, k * LANES : (k + 1) * LANES] = cos.astype(BF16)
            far = k + turns // 2
            table_ref[here, far * LANES : (far + 1) * LANES] = (cos * half_turn).astype(BF16)
            cos, sin = cos * turn_cos - sin * turn_sin, sin * turn_cos + cos * turn_sin


def sent_kernel(
    slots, y_count, place_ref, freq_ref, velocity_ref, matrix_ref,
    out_ref, freq_in, velocity_in, matrix_in, table, sems,
):
    copies = [
        pltpu.make_async_copy(freq_ref, freq_in, sems.at[0]),
        pltpu.make_async_copy(velocity_ref, velocity_in, sems.at[1]),
        pltpu.make_async_copy(matrix_ref, matrix_in, sems.at[2]),
    ]
    for copy in copies:
        copy.start()
    copies[0].wait()
    make_table(slots, y_count, 1 - place_ref[0], freq_in, table)
    copies[1].wait()
    out_ref[...] = dot_t(table[...], velocity_in[...]).astype(BF16)
    copies[2].wait()


def own_kernel(
    slots, y_count, place_ref, freq_ref, velocity_ref, matrix_ref, table_ref, out_ref, rounded_ref
):
    rounded_ref[...] = matrix_ref[...].astype(BF16)
    make_table(slots, y_count, place_ref[0], freq_ref, table_ref)
    out_ref[...] = dot_t(table_ref[...], velocity_ref[...]).astype(BF16)


def in_hbm(value):
    return pltpu.with_memory_space_constraint(value, pltpu.HBM)


def make_spectra(place, freq_table, velocity, matrix):
    y_count, cores = lax.axis_size(Y), lax.axis_size(CORE)
    all_slots = freq_table.shape[0]
    slots = all_slots // (lax.axis_size(Z) * y_count * cores)
    patches, steps = velocity.shape
    assert 8 * LANES == steps and slots & (slots - 1) == 0 and cores == 2
    rows = 2 * all_slots // cores
    hbm = pl.BlockSpec(memory_space=pltpu.HBM)
    table, spectra = shape((rows, steps), BF16), shape((rows, patches), BF16)
    sent, freq, velocity, matrix = call(
        functools.partial(sent_kernel, slots, y_count),
        (
            spectra,
            shape((1, all_slots), I32),
            shape(velocity.shape, BF16),
            shape(matrix.shape, F32),
        ),
        1,
        1,
        in_specs=[SMEM, hbm, hbm, hbm],
        out_specs=(WHOLE, WHOLE, WHOLE, WHOLE),
        scratch_shapes=[pltpu.VMEM((rows, steps), BF16), pltpu.SemaphoreType.DMA((3,))],
    )(place, in_hbm(freq_table.reshape(1, -1)), in_hbm(velocity), in_hbm(matrix))
    own = call(
        functools.partial(own_kernel, slots, y_count),
        (table, spectra, shape(matrix.shape, BF16)),
        1,
        1,
        in_specs=[SMEM, WHOLE, WHOLE, WHOLE],
        out_specs=(WHOLE, WHOLE, WHOLE),
    )(place, freq, velocity, matrix)
    return sent, *own


def partial_kernel(spectra_ref, basis_ref, before_ref, out_ref):
    for k in range(basis_ref.shape[0]):
        out_ref[k] = (dot(spectra_ref[...], basis_ref[k]) + before_ref[k]).astype(BF16)


def make_partial(spectra, basis, before):
    return call(
        partial_kernel,
        shape(before.shape, BF16),
        2 * before.size * spectra.shape[1],
        in_specs=[WHOLE] * 3,
        out_specs=WHOLE,
    )(spectra, basis, before)


def first_kernel(spectra_ref, basis_ref, out_ref):
    for k in range(basis_ref.shape[0]):
        out_ref[k] = dot(spectra_ref[...], basis_ref[k])


def first_partial(spectra, basis):
    rows, patches = spectra.shape
    parts, _, width = basis.shape
    return call(
        first_kernel,
        shape((parts, rows, width), F32),
        2 * rows * patches * parts * width,
        in_specs=[WHOLE, WHOLE],
        out_specs=WHOLE,
    )(spectra, basis)


def added(parts_ref):
    total = parts_ref[0].astype(F32)
    for k in range(1, parts_ref.shape[0]):
        total = total + parts_ref[k].astype(F32)
    return total


def sum_kernel(parts_ref, out_ref):
    out_ref[...] = added(parts_ref).astype(BF16)


def summed(parts):
    return call(
        sum_kernel, shape(parts.shape[1:], BF16), parts.size, in_specs=[WHOLE], out_specs=WHOLE
    )(parts)


def kept(value, limit_ref):
    index = lax.broadcasted_iota(I32, value.shape, 1)
    return jnp.where(index < limit_ref[:1, :1], value, 0.0)


def coefficients_kernel(limit_ref, parts_ref, out_ref):
    value = kept(added(parts_ref), limit_ref).astype(BF16)
    out_ref[...] = jnp.broadcast_to(value, out_ref.shape)


def make_coefficients(limit, parts, copies):
    return call(
        coefficients_kernel,
        shape((copies, *parts.shape[1:]), BF16),
        parts.size,
        in_specs=[WHOLE, WHOLE],
        out_specs=WHOLE,
    )(limit, parts)


def forcing_kernel(limit_ref, coef_ref, matrix_ref, out_ref):
    width = coef_ref.shape[2]
    total = dot(coef_ref[0], matrix_ref[:width])
    for k in range(1, coef_ref.shape[0]):
        total = total + dot(coef_ref[k], matrix_ref[k * width : (k + 1) * width])
    value = kept(2.0 * total, limit_ref).astype(BF16)
    out_ref[...] = jnp.broadcast_to(value, out_ref.shape)


def make_forcing(limit, coef, matrix, copies):
    rows = coef.shape[1]
    return call(
        forcing_kernel,
        shape((copies, rows, matrix.shape[1]), BF16),
        2 * rows * matrix.size,
        in_specs=[WHOLE, WHOLE, WHOLE],
        out_specs=WHOLE,
    )(limit, coef, matrix)


def history_kernel(basis_ref, forcing_ref, table_ref, *rest):
    out_ref = rest[-1]
    total = dot_t(basis_ref[0], forcing_ref[0])
    for k in range(1, basis_ref.shape[0]):
        total = total + dot_t(basis_ref[k], forcing_ref[k])
    out_ref[...] = dot(total.astype(BF16), table_ref[...]).astype(out_ref.dtype)


def make_history(basis, forcing, table, dtype):
    parts, patches, width = basis.shape
    rows = forcing.shape[1]
    steps = table.shape[1]
    return call(
        history_kernel,
        shape((patches, steps), dtype),
        2 * rows * patches * (steps + parts * width),
        in_specs=[WHOLE, WHOLE, WHOLE],
        out_specs=WHOLE,
    )(basis, forcing, table)


def finish_kernel(own_ref, received_ref, out_ref, done, sems):
    pieces = sems.shape[0]
    rows = own_ref.shape[0] // pieces
    copies = []
    for k in range(pieces):
        here = pl.ds(k * rows, rows)
        done[here] = (own_ref[here] + received_ref[here].astype(F32)).astype(BF16)
        copies.append(pltpu.make_async_copy(done.at[here], out_ref.at[here], sems.at[k]))
        copies[-1].start()
    for copy in copies:
        copy.wait()


def finish(own, received):
    return call(
        finish_kernel,
        shape(own.shape, BF16),
        own.size,
        in_specs=[WHOLE, WHOLE],
        out_specs=pl.BlockSpec(memory_space=pltpu.HBM),
        scratch_shapes=[pltpu.VMEM(own.shape, BF16), pltpu.SemaphoreType.DMA((4,))],
    )(own, received)


def exchange(value, axis):
    return lax.all_to_all(value, axis, split_axis=0, concat_axis=0, tiled=True)


def swap_cores(value):
    return lax.ppermute(value, CORE, [(0, 1), (1, 0)])


def per_device(velocity, radiation_modes, resistance, mode_ranks, freq_table):
    modes, ys, zs = lax.axis_size(MODE), lax.axis_size(Y), lax.axis_size(Z)
    width = radiation_modes.shape[1]
    place = lax.axis_index(CORE).reshape(1)
    basis = exchange(radiation_modes.reshape(modes, -1, width), MODE)
    sent, table, spectra, matrix = make_spectra(place, freq_table, velocity[0], resistance[0])
    spectra_other = swap_cores(sent)
    limit = jnp.broadcast_to(mode_ranks[0] - lax.axis_index(MODE) * width, (8, LANES))
    basis, spectra, spectra_other, limit = lax.optimization_barrier(
        (basis, spectra, spectra_other, limit)
    )
    basis_other = swap_cores(basis)
    coef = first_partial(spectra, basis)
    coef = make_partial(spectra_other, basis_other, coef)
    coef = summed(exchange(coef.reshape(modes * ys, -1, width), (MODE, Y)))
    coef = exchange(coef.reshape(zs, -1, width), Z)
    coef = exchange(make_coefficients(limit, coef, modes), MODE)
    forcing = exchange(make_forcing(limit, coef, matrix, zs), Z)
    forcing = forcing.reshape(-1, width)
    forcing = exchange(jnp.broadcast_to(forcing, (modes * ys, *forcing.shape)), (MODE, Y))
    forcing = forcing.reshape(modes, -1, width)
    received = swap_cores(make_history(basis_other, forcing, table, BF16))
    history = make_history(basis, forcing, table, F32)
    return finish(history, received)[None]


def solution(mesh):
    torus = Mesh(mesh.devices.reshape(16, 4, 2, mesh.shape["mode"]), (Z, Y, CORE, MODE))
    bands = (Z, Y, CORE)
    patches = (Z, Y, CORE, MODE)
    in_specs = (P(None, patches, None), P(bands, MODE), P(bands, None, MODE), P(bands), P())
    return jax.shard_map(
        per_device, mesh=torus, in_specs=in_specs, out_specs=P(None, patches, None), check_vma=False
    )
```

```python
import functools
import math

import jax
import jax.numpy as jnp
from jax import lax
from jax.experimental import pallas as pl
from jax.experimental.pallas import tpu as pltpu
from jax.sharding import Mesh
from jax.sharding import PartitionSpec as P

Z, Y, CORE, MODE = "band_0", "band_1", "band_2", "mode"
F32, BF16, I32 = jnp.float32, jnp.bfloat16, jnp.int32
LANES = 128
VMEM_BYTES = 24 * 1024 * 1024
WHOLE = pl.BlockSpec(memory_space=pltpu.VMEM)


def shape(dims, dtype):
    return jax.ShapeDtypeStruct(tuple(dims), dtype)


def call(kernel, out_shape, flops, bytes_accessed=1 << 20, **options):
    return pl.pallas_call(
        kernel,
        out_shape=out_shape,
        compiler_params=pltpu.CompilerParams(vmem_limit_bytes=VMEM_BYTES),
        cost_estimate=pl.CostEstimate(
            flops=flops, bytes_accessed=bytes_accessed, transcendentals=0
        ),
        **options,
    )


def dot(a, b):
    return jnp.dot(a, b, preferred_element_type=F32)


def dot_t(a, b):
    return lax.dot_general(a, b, (((1,), (1,)), ((), ())), preferred_element_type=F32)


def sin_cos(phase, steps):
    quadrant = (phase + steps // 8) >> (int(math.log2(steps)) - 2)
    x = (phase - quadrant * (steps // 4)).astype(F32) * (2.0 * math.pi / steps)
    y = x * x
    sin = x * (1.0 + y * (-1 / 6 + y * (1 / 120 + y * (-1 / 5040 + y * (1 / 362880)))))
    cos = 1.0 + y * (-1 / 2 + y * (1 / 24 + y * (-1 / 720 + y * (1 / 40320 - y * (1 / 3628800)))))
    odd = (quadrant & 1) == 1
    sign_sin = jnp.where((quadrant & 2) == 2, -1.0, 1.0)
    sign_cos = jnp.where(((quadrant + 1) & 2) == 2, -1.0, 1.0)
    return jnp.where(odd, cos, sin) * sign_sin, jnp.where(odd, sin, cos) * sign_cos


def cos_eighth(k):
    size = jnp.where((k & 1) == 1, math.sqrt(0.5), jnp.where((k & 2) == 2, 0.0, 1.0))
    return jnp.where(((k + 1) & 4) == 4, -size, size)


def make_table(slots, y_count, core, freq_in, table_ref):
    all_rows, steps = table_ref.shape
    all_slots = freq_in.shape[1]
    rows = all_rows // y_count
    cores = 2 * all_slots // all_rows
    shift = int(math.log2(slots))
    turns = steps // LANES
    norming = 1.0 / math.sqrt(steps)
    row = lax.broadcasted_iota(I32, (rows, 1), 0)
    first = (row >> (shift + 1)) * (y_count * cores * slots) + (row & (slots - 1)) + core * slots
    lane = lax.broadcasted_iota(I32, (rows, all_slots), 1)
    low = lax.broadcasted_iota(I32, (rows, LANES), 1)
    quarter = ((row >> shift) & 1) * (steps // 4)
    for y in range(y_count):
        here = slice(y * rows, (y + 1) * rows)
        freq = jnp.where(lane == first + y * cores * slots, freq_in[...].astype(F32), 0.0)
        freq = jnp.sum(freq, axis=1, keepdims=True).astype(I32)
        freq = jnp.broadcast_to(freq, (rows, LANES))
        sin, cos = sin_cos((low * freq + quarter) & (steps - 1), steps)
        sin, cos = sin * norming, cos * norming
        turn_cos, turn_sin = cos_eighth(freq & 7), cos_eighth((freq + 6) & 7)
        half_turn = jnp.where((freq & 1) == 1, -1.0, 1.0)
        for k in range(turns // 2):
            table_ref[here, k * LANES : (k + 1) * LANES] = cos.astype(BF16)
            far = k + turns // 2
            table_ref[here, far * LANES : (far + 1) * LANES] = (cos * half_turn).astype(BF16)
            cos, sin = cos * turn_cos - sin * turn_sin, sin * turn_cos + cos * turn_sin


def sent_kernel(
    slots, y_count, freq_ref, velocity_ref, matrix_ref,
    out_ref, freq_in, velocity_in, matrix_in, table, sems,
):
    copies = [
        pltpu.make_async_copy(freq_ref, freq_in, sems.at[0]),
        pltpu.make_async_copy(velocity_ref, velocity_in, sems.at[1]),
        pltpu.make_async_copy(matrix_ref, matrix_in, sems.at[2]),
    ]
    for copy in copies:
        copy.start()
    copies[0].wait()
    make_table(slots, y_count, 1 - lax.axis_index(CORE), freq_in, table)
    copies[1].wait()
    out_ref[...] = dot_t(table[...], velocity_in[...]).astype(BF16)
    copies[2].wait()


def own_kernel(
    slots, y_count, freq_ref, velocity_ref, matrix_ref, table_ref, out_ref, rounded_ref
):
    rounded_ref[...] = matrix_ref[...].astype(BF16)
    make_table(slots, y_count, lax.axis_index(CORE), freq_ref, table_ref)
    out_ref[...] = dot_t(table_ref[...], velocity_ref[...]).astype(BF16)


def in_hbm(value):
    return pltpu.with_memory_space_constraint(value, pltpu.HBM)


def make_spectra(freq_table, velocity, matrix):
    y_count, cores = lax.axis_size(Y), lax.axis_size(CORE)
    all_slots = freq_table.shape[0]
    slots = all_slots // (lax.axis_size(Z) * y_count * cores)
    patches, steps = velocity.shape
    assert 8 * LANES == steps and slots & (slots - 1) == 0 and cores == 2
    rows = 2 * all_slots // cores
    hbm = pl.BlockSpec(memory_space=pltpu.HBM)
    table, spectra = shape((rows, steps), BF16), shape((rows, patches), BF16)
    sent, freq, velocity, matrix = call(
        functools.partial(sent_kernel, slots, y_count),
        (
            spectra,
            shape((1, all_slots), I32),
            shape(velocity.shape, BF16),
            shape(matrix.shape, F32),
        ),
        1,
        1,
        in_specs=[hbm, hbm, hbm],
        out_specs=(WHOLE, WHOLE, WHOLE, WHOLE),
        scratch_shapes=[pltpu.VMEM((rows, steps), BF16), pltpu.SemaphoreType.DMA((3,))],
    )(in_hbm(freq_table.reshape(1, -1)), in_hbm(velocity), in_hbm(matrix))
    own = call(
        functools.partial(own_kernel, slots, y_count),
        (table, spectra, shape(matrix.shape, BF16)),
        1,
        1,
        in_specs=[WHOLE, WHOLE, WHOLE],
        out_specs=(WHOLE, WHOLE, WHOLE),
    )(freq, velocity, matrix)
    return sent, *own


def partial_kernel(spectra_ref, basis_ref, before_ref, out_ref):
    for k in range(basis_ref.shape[0]):
        out_ref[k] = (dot(spectra_ref[...], basis_ref[k]) + before_ref[k]).astype(BF16)


def make_partial(spectra, basis, before):
    return call(
        partial_kernel,
        shape(before.shape, BF16),
        2 * before.size * spectra.shape[1],
        in_specs=[WHOLE] * 3,
        out_specs=WHOLE,
    )(spectra, basis, before)


def first_kernel(spectra_ref, basis_ref, out_ref):
    for k in range(basis_ref.shape[0]):
        out_ref[k] = dot(spectra_ref[...], basis_ref[k])


def first_partial(spectra, basis):
    rows, patches = spectra.shape
    parts, _, width = basis.shape
    return call(
        first_kernel,
        shape((parts, rows, width), F32),
        2 * rows * patches * parts * width,
        in_specs=[WHOLE, WHOLE],
        out_specs=WHOLE,
    )(spectra, basis)


def added(parts_ref):
    total = parts_ref[0].astype(F32)
    for k in range(1, parts_ref.shape[0]):
        total = total + parts_ref[k].astype(F32)
    return total


def sum_kernel(parts_ref, out_ref):
    out_ref[...] = added(parts_ref).astype(BF16)


def summed(parts):
    return call(
        sum_kernel, shape(parts.shape[1:], BF16), parts.size, in_specs=[WHOLE], out_specs=WHOLE
    )(parts)


def kept(value, limit_ref):
    index = lax.broadcasted_iota(I32, value.shape, 1)
    return jnp.where(index < limit_ref[:1, :1], value, 0.0)


def coefficients_kernel(limit_ref, parts_ref, out_ref):
    value = kept(added(parts_ref), limit_ref).astype(BF16)
    out_ref[...] = jnp.broadcast_to(value, out_ref.shape)


def make_coefficients(limit, parts, copies):
    return call(
        coefficients_kernel,
        shape((copies, *parts.shape[1:]), BF16),
        parts.size,
        in_specs=[WHOLE, WHOLE],
        out_specs=WHOLE,
    )(limit, parts)


def forcing_kernel(limit_ref, coef_ref, matrix_ref, out_ref):
    width = coef_ref.shape[2]
    total = dot(coef_ref[0], matrix_ref[:width])
    for k in range(1, coef_ref.shape[0]):
        total = total + dot(coef_ref[k], matrix_ref[k * width : (k + 1) * width])
    value = kept(2.0 * total, limit_ref).astype(BF16)
    out_ref[...] = jnp.broadcast_to(value, out_ref.shape)


def make_forcing(limit, coef, matrix, copies):
    rows = coef.shape[1]
    return call(
        forcing_kernel,
        shape((copies, rows, matrix.shape[1]), BF16),
        2 * rows * matrix.size,
        in_specs=[WHOLE, WHOLE, WHOLE],
        out_specs=WHOLE,
    )(limit, coef, matrix)


def history_kernel(basis_ref, forcing_ref, table_ref, *rest):
    out_ref = rest[-1]
    total = dot_t(basis_ref[0], forcing_ref[0])
    for k in range(1, basis_ref.shape[0]):
        total = total + dot_t(basis_ref[k], forcing_ref[k])
    out_ref[...] = dot(total.astype(BF16), table_ref[...]).astype(out_ref.dtype)


def make_history(basis, forcing, table, dtype):
    parts, patches, width = basis.shape
    rows = forcing.shape[1]
    steps = table.shape[1]
    return call(
        history_kernel,
        shape((patches, steps), dtype),
        2 * rows * patches * (steps + parts * width),
        grid=(1,),
        in_specs=[
            pl.BlockSpec(basis.shape, lambda i: (0, 0, 0)),
            pl.BlockSpec(forcing.shape, lambda i: (0, 0, 0)),
            pl.BlockSpec((rows, steps), lambda i: (0, 0)),
        ],
        out_specs=pl.BlockSpec((patches, steps), lambda i: (0, 0)),
    )(basis, forcing, table)


def exchange(value, axis):
    return lax.all_to_all(value, axis, split_axis=0, concat_axis=0, tiled=True)


def swap_cores(value):
    return lax.ppermute(value, CORE, [(0, 1), (1, 0)])


def per_device(velocity, radiation_modes, resistance, mode_ranks, freq_table):
    modes, ys, zs = lax.axis_size(MODE), lax.axis_size(Y), lax.axis_size(Z)
    width = radiation_modes.shape[1]
    basis = exchange(radiation_modes.reshape(modes, -1, width), MODE)
    sent, table, spectra, matrix = make_spectra(freq_table, velocity[0], resistance[0])
    spectra_other = swap_cores(sent)
    limit = jnp.broadcast_to(mode_ranks[0] - lax.axis_index(MODE) * width, (8, LANES))
    basis, spectra, spectra_other, limit = lax.optimization_barrier(
        (basis, spectra, spectra_other, limit)
    )
    basis_other = swap_cores(basis)
    coef = first_partial(spectra, basis)
    coef = make_partial(spectra_other, basis_other, coef)
    coef = summed(exchange(coef.reshape(modes * ys, -1, width), (MODE, Y)))
    coef = exchange(coef.reshape(zs, -1, width), Z)
    coef = exchange(make_coefficients(limit, coef, modes), MODE)
    forcing = exchange(make_forcing(limit, coef, matrix, zs), Z)
    forcing = forcing.reshape(-1, width)
    forcing = exchange(jnp.broadcast_to(forcing, (modes * ys, *forcing.shape)), (MODE, Y))
    forcing = forcing.reshape(modes, -1, width)
    received = swap_cores(make_history(basis_other, forcing, table, BF16))
    history = make_history(basis, forcing, table, F32)
    return (history + received.astype(F32)).astype(BF16)[None]


def solution(mesh):
    torus = Mesh(mesh.devices.reshape(16, 4, 2, mesh.shape["mode"]), (Z, Y, CORE, MODE))
    bands = (Z, Y, CORE)
    patches = (Z, Y, CORE, MODE)
    in_specs = (P(None, patches, None), P(bands, MODE), P(bands, None, MODE), P(bands), P())
    return jax.shard_map(
        per_device, mesh=torus, in_specs=in_specs, out_specs=P(None, patches, None), check_vma=False
    )
```

```python
import functools
import math

import jax
import jax.numpy as jnp
from jax import lax
from jax.experimental import pallas as pl
from jax.experimental.pallas import tpu as pltpu
from jax.sharding import Mesh
from jax.sharding import PartitionSpec as P

Z, Y, CORE, MODE = "band_0", "band_1", "band_2", "mode"
F32, BF16, I32 = jnp.float32, jnp.bfloat16, jnp.int32
LANES = 128
VMEM_BYTES = 24 * 1024 * 1024
SMEM = pl.BlockSpec(memory_space=pltpu.SMEM)
WHOLE = pl.BlockSpec(memory_space=pltpu.VMEM)


def shape(dims, dtype):
    return jax.ShapeDtypeStruct(tuple(dims), dtype)


def call(kernel, out_shape, flops, bytes_accessed=1 << 20, **options):
    return pl.pallas_call(
        kernel,
        out_shape=out_shape,
        compiler_params=pltpu.CompilerParams(vmem_limit_bytes=VMEM_BYTES),
        cost_estimate=pl.CostEstimate(
            flops=flops, bytes_accessed=bytes_accessed, transcendentals=0
        ),
        **options,
    )


def dot(a, b):
    return jnp.dot(a, b, preferred_element_type=F32)


def dot_t(a, b):
    return lax.dot_general(a, b, (((1,), (1,)), ((), ())), preferred_element_type=F32)


def sin_cos(phase, steps):
    quadrant = (phase + steps // 8) >> (int(math.log2(steps)) - 2)
    x = (phase - quadrant * (steps // 4)).astype(F32) * (2.0 * math.pi / steps)
    y = x * x
    sin = x * (1.0 + y * (-1 / 6 + y * (1 / 120 + y * (-1 / 5040 + y * (1 / 362880)))))
    cos = 1.0 + y * (-1 / 2 + y * (1 / 24 + y * (-1 / 720 + y * (1 / 40320 - y * (1 / 3628800)))))
    odd = (quadrant & 1) == 1
    sign_sin = jnp.where((quadrant & 2) == 2, -1.0, 1.0)
    sign_cos = jnp.where(((quadrant + 1) & 2) == 2, -1.0, 1.0)
    return jnp.where(odd, cos, sin) * sign_sin, jnp.where(odd, sin, cos) * sign_cos


def cos_eighth(k):
    size = jnp.where((k & 1) == 1, math.sqrt(0.5), jnp.where((k & 2) == 2, 0.0, 1.0))
    return jnp.where(((k + 1) & 4) == 4, -size, size)


def make_table(slots, y_count, core, freq_in, table_ref):
    all_rows, steps = table_ref.shape
    all_slots = freq_in.shape[1]
    rows = all_rows // y_count
    cores = 2 * all_slots // all_rows
    shift = int(math.log2(slots))
    turns = steps // LANES
    norming = 1.0 / math.sqrt(steps)
    row = lax.broadcasted_iota(I32, (rows, 1), 0)
    first = (row >> (shift + 1)) * (y_count * cores * slots) + (row & (slots - 1)) + core * slots
    lane = lax.broadcasted_iota(I32, (rows, all_slots), 1)
    low = lax.broadcasted_iota(I32, (rows, LANES), 1)
    quarter = ((row >> shift) & 1) * (steps // 4)
    for y in range(y_count):
        here = slice(y * rows, (y + 1) * rows)
        freq = jnp.where(lane == first + y * cores * slots, freq_in[...].astype(F32), 0.0)
        freq = jnp.sum(freq, axis=1, keepdims=True).astype(I32)
        freq = jnp.broadcast_to(freq, (rows, LANES))
        sin, cos = sin_cos((low * freq + quarter) & (steps - 1), steps)
        sin, cos = sin * norming, cos * norming
        turn_cos, turn_sin = cos_eighth(freq & 7), cos_eighth((freq + 6) & 7)
        half_turn = jnp.where((freq & 1) == 1, -1.0, 1.0)
        for k in range(turns // 2):
            table_ref[here, k * LANES : (k + 1) * LANES] = cos.astype(BF16)
            far = k + turns // 2
            table_ref[here, far * LANES : (far + 1) * LANES] = (cos * half_turn).astype(BF16)
            cos, sin = cos * turn_cos - sin * turn_sin, sin * turn_cos + cos * turn_sin


def sent_kernel(
    slots, y_count, place_ref, freq_ref, velocity_ref, matrix_ref,
    out_ref, freq_in, velocity_in, matrix_in, table, sems,
):
    copies = [
        pltpu.make_async_copy(freq_ref, freq_in, sems.at[0]),
        pltpu.make_async_copy(velocity_ref, velocity_in, sems.at[1]),
        pltpu.make_async_copy(matrix_ref, matrix_in, sems.at[2]),
    ]
    for copy in copies:
        copy.start()
    copies[0].wait()
    make_table(slots, y_count, 1 - place_ref[0], freq_in, table)
    copies[1].wait()
    out_ref[...] = dot_t(table[...], velocity_in[...]).astype(BF16)
    copies[2].wait()


def own_kernel(
    slots, y_count, place_ref, freq_ref, velocity_ref, matrix_ref, table_ref, out_ref, rounded_ref
):
    rounded_ref[...] = matrix_ref[...].astype(BF16)
    make_table(slots, y_count, place_ref[0], freq_ref, table_ref)
    out_ref[...] = dot_t(table_ref[...], velocity_ref[...]).astype(BF16)


def in_hbm(value):
    return pltpu.with_memory_space_constraint(value, pltpu.HBM)


def make_spectra(place, freq_table, velocity, matrix):
    y_count, cores = lax.axis_size(Y), lax.axis_size(CORE)
    all_slots = freq_table.shape[0]
    slots = all_slots // (lax.axis_size(Z) * y_count * cores)
    patches, steps = velocity.shape
    assert 8 * LANES == steps and slots & (slots - 1) == 0 and cores == 2
    rows = 2 * all_slots // cores
    hbm = pl.BlockSpec(memory_space=pltpu.HBM)
    table, spectra = shape((rows, steps), BF16), shape((rows, patches), BF16)
    sent, freq, velocity, matrix = call(
        functools.partial(sent_kernel, slots, y_count),
        (
            spectra,
            shape((1, all_slots), I32),
            shape(velocity.shape, BF16),
            shape(matrix.shape, F32),
        ),
        1,
        1,
        in_specs=[SMEM, hbm, hbm, hbm],
        out_specs=(WHOLE, WHOLE, WHOLE, WHOLE),
        scratch_shapes=[pltpu.VMEM((rows, steps), BF16), pltpu.SemaphoreType.DMA((3,))],
    )(place, in_hbm(freq_table.reshape(1, -1)), in_hbm(velocity), in_hbm(matrix))
    own = call(
        functools.partial(own_kernel, slots, y_count),
        (table, spectra, shape(matrix.shape, BF16)),
        1,
        1,
        in_specs=[SMEM, WHOLE, WHOLE, WHOLE],
        out_specs=(WHOLE, WHOLE, WHOLE),
    )(place, freq, velocity, matrix)
    return sent, *own


def partial_kernel(spectra_ref, basis_ref, before_ref, out_ref):
    for k in range(basis_ref.shape[0]):
        out_ref[k] = (dot(spectra_ref[...], basis_ref[k]) + before_ref[k]).astype(BF16)


def make_partial(spectra, basis, before):
    return call(
        partial_kernel,
        shape(before.shape, BF16),
        2 * before.size * spectra.shape[1],
        in_specs=[WHOLE] * 3,
        out_specs=WHOLE,
    )(spectra, basis, before)


def first_kernel(spectra_ref, basis_ref, out_ref):
    for k in range(basis_ref.shape[0]):
        out_ref[k] = dot(spectra_ref[...], basis_ref[k])


def first_partial(spectra, basis):
    rows, patches = spectra.shape
    parts, _, width = basis.shape
    return call(
        first_kernel,
        shape((parts, rows, width), F32),
        2 * rows * patches * parts * width,
        in_specs=[WHOLE, WHOLE],
        out_specs=WHOLE,
    )(spectra, basis)


def added(parts_ref):
    total = parts_ref[0].astype(F32)
    for k in range(1, parts_ref.shape[0]):
        total = total + parts_ref[k].astype(F32)
    return total


def sum_kernel(parts_ref, out_ref):
    out_ref[...] = added(parts_ref).astype(BF16)


def summed(parts):
    return call(
        sum_kernel, shape(parts.shape[1:], BF16), parts.size, in_specs=[WHOLE], out_specs=WHOLE
    )(parts)


def kept(value, limit_ref):
    index = lax.broadcasted_iota(I32, value.shape, 1)
    return jnp.where(index < limit_ref[:1, :1], value, 0.0)


def coefficients_kernel(limit_ref, parts_ref, out_ref):
    value = kept(added(parts_ref), limit_ref).astype(BF16)
    out_ref[...] = jnp.broadcast_to(value, out_ref.shape)


def make_coefficients(limit, parts, copies):
    return call(
        coefficients_kernel,
        shape((copies, *parts.shape[1:]), BF16),
        parts.size,
        in_specs=[WHOLE, WHOLE],
        out_specs=WHOLE,
    )(limit, parts)


def forcing_kernel(limit_ref, coef_ref, matrix_ref, out_ref):
    width = coef_ref.shape[2]
    total = dot(coef_ref[0], matrix_ref[:width])
    for k in range(1, coef_ref.shape[0]):
        total = total + dot(coef_ref[k], matrix_ref[k * width : (k + 1) * width])
    value = kept(2.0 * total, limit_ref).astype(BF16)
    out_ref[...] = jnp.broadcast_to(value, out_ref.shape)


def make_forcing(limit, coef, matrix, copies):
    rows = coef.shape[1]
    return call(
        forcing_kernel,
        shape((copies, rows, matrix.shape[1]), BF16),
        2 * rows * matrix.size,
        in_specs=[WHOLE, WHOLE, WHOLE],
        out_specs=WHOLE,
    )(limit, coef, matrix)


def history_kernel(basis_ref, forcing_ref, table_ref, *rest):
    out_ref = rest[-1]
    blocks = range(basis_ref.shape[0])
    basis = jnp.concatenate([basis_ref[k] for k in blocks], axis=1)
    total = dot_t(basis, jnp.concatenate([forcing_ref[k] for k in blocks], axis=1))
    out_ref[...] = dot(total.astype(BF16), table_ref[...]).astype(out_ref.dtype)


def make_history(basis, forcing, table, dtype):
    parts, patches, width = basis.shape
    rows = forcing.shape[1]
    steps = table.shape[1]
    return call(
        history_kernel,
        shape((patches, steps), dtype),
        2 * rows * patches * (steps + parts * width),
        grid=(1,),
        in_specs=[
            pl.BlockSpec(basis.shape, lambda i: (0, 0, 0)),
            pl.BlockSpec(forcing.shape, lambda i: (0, 0, 0)),
            pl.BlockSpec((rows, steps), lambda i: (0, 0)),
        ],
        out_specs=pl.BlockSpec((patches, steps), lambda i: (0, 0)),
    )(basis, forcing, table)


def exchange(value, axis):
    return lax.all_to_all(value, axis, split_axis=0, concat_axis=0, tiled=True)


def swap_cores(value):
    return lax.ppermute(value, CORE, [(0, 1), (1, 0)])


def per_device(velocity, radiation_modes, resistance, mode_ranks, freq_table):
    modes, ys, zs = lax.axis_size(MODE), lax.axis_size(Y), lax.axis_size(Z)
    width = radiation_modes.shape[1]
    place = lax.axis_index(CORE).reshape(1)
    basis = exchange(radiation_modes.reshape(modes, -1, width), MODE)
    sent, table, spectra, matrix = make_spectra(place, freq_table, velocity[0], resistance[0])
    spectra_other = swap_cores(sent)
    limit = jnp.broadcast_to(mode_ranks[0] - lax.axis_index(MODE) * width, (8, LANES))
    basis, spectra, spectra_other, limit = lax.optimization_barrier(
        (basis, spectra, spectra_other, limit)
    )
    basis_other = swap_cores(basis)
    coef = first_partial(spectra, basis)
    coef = make_partial(spectra_other, basis_other, coef)
    coef = summed(exchange(coef.reshape(modes * ys, -1, width), (MODE, Y)))
    coef = exchange(coef.reshape(zs, -1, width), Z)
    coef = exchange(make_coefficients(limit, coef, modes), MODE)
    forcing = exchange(make_forcing(limit, coef, matrix, zs), Z)
    forcing = forcing.reshape(-1, width)
    forcing = exchange(jnp.broadcast_to(forcing, (modes * ys, *forcing.shape)), (MODE, Y))
    forcing = forcing.reshape(modes, -1, width)
    received = swap_cores(make_history(basis_other, forcing, table, BF16))
    history = make_history(basis, forcing, table, F32)
    return (history + received.astype(F32)).astype(BF16)[None]


def solution(mesh):
    torus = Mesh(mesh.devices.reshape(16, 4, 2, mesh.shape["mode"]), (Z, Y, CORE, MODE))
    bands = (Z, Y, CORE)
    patches = (Z, Y, CORE, MODE)
    in_specs = (P(None, patches, None), P(bands, MODE), P(bands, None, MODE), P(bands), P())
    return jax.shard_map(
        per_device, mesh=torus, in_specs=in_specs, out_specs=P(None, patches, None), check_vma=False
    )
```
